32 devices in a mesh: clu: 16 (over z, y, core), col: 2 (over x).
Axes of the slice: x: 2, y: 2, z: 4, core: 2. Of those that a mesh axis runs over, the one named last changes fastest.
Arguments:
- near_blocks: float32 [16, 16, 512, 512], P('clu', 'col'), may hold values from -0.25 to 0.25
- diag_block: float32 [16, 512, 512], P('clu', 'col'), as said below
- bases: float32 [16, 512, 512], P('clu', 'col'), as said below
- near_index: int32 [16, 16], replicated, may hold values from 0 to 15, as said below
- near_mask: int32 [16, 16], P('clu'), may hold values from 0 to 1
- parent_map: int32 [16], replicated, may hold values from 0 to 7, as said below
Outputs:
- coupling: float32 [16, 16, 256, 256], P('clu', 'col')
- parent_rows: float32 [16, 256, 512], P('clu', 'col')
- redundant_factor: float32 [16, 256, 256], P('clu', 'col')
The draws below stay inside these ranges and needn't reach their ends.
Inputs may be any that keep to these rules, and one draw needn't show every extreme that they name: `parent_map`: every parent has exactly two children. `near_index`: the slots of cluster i name the clusters (i + d) mod 16 for d = 1 to 7, d = 8 and d = -1 to -8, each offset in exactly one slot, in an order drawn per row; live slots name distinct clusters; exactly one live slot names the cluster's sibling. `diag_block`: each block is symmetric and positive definite. `bases`: each basis change is invertible.
All inputs are finite; a program needn't handle non-finite values.
Results may differ from the reference program's by a relative error of at most 0.0003.
Values sent between devices are 32-bit elements; how exact they have to be, the bound alone decides.
A program may use at most 64 MiB of HBM per device.

```python
import jax
import jax.numpy as jnp
from jax import lax

LEAF = 512
NEAR = 16
RED = 256
CLUSTERS = 16


def near_tables(key):
    base = jax.random.fold_in(key, 4242)
    key_pair, key_order, key_live = jax.random.split(base, 3)
    cluster_ids = jnp.arange(CLUSTERS, dtype=jnp.int32)
    groups = CLUSTERS // 4
    pair_keys = jax.random.split(key_pair, groups)
    inner = jax.vmap(lambda subkey: jax.random.permutation(subkey, 4))(pair_keys).astype(jnp.int32)
    members = (jnp.arange(groups, dtype=jnp.int32)[:, None] * 4 + inner).reshape(-1)
    position = jnp.zeros((CLUSTERS,), jnp.int32).at[members].set(cluster_ids)
    parent = position // 2
    partner_pos = position + 1 - 2 * (position % 2)
    sibling = members[partner_pos]
    half = NEAR // 2
    far = CLUSTERS // 2
    steps_up = jnp.arange(1, half, dtype=jnp.int32)
    steps_down = jnp.arange(1, half + 1, dtype=jnp.int32)
    offset_table = jnp.concatenate([steps_up, jnp.full((1,), far, jnp.int32), -steps_down])
    row_keys = jax.random.split(key_order, CLUSTERS)
    orders = jax.vmap(lambda subkey: jax.random.permutation(subkey, NEAR))(row_keys).astype(jnp.int32)
    chosen = offset_table[orders]
    near = (cluster_ids[:, None] + chosen) % CLUSTERS
    wanted = (sibling - cluster_ids + CLUSTERS) % CLUSTERS
    is_sibling = (chosen + CLUSTERS) % CLUSTERS == wanted[:, None]
    repeat = (chosen == far) & (far == half)
    coins = jax.random.randint(key_live, (CLUSTERS, NEAR), 0, 4)
    live = ((coins != 0) | is_sibling) & jnp.logical_not(repeat)
    return (near.astype(jnp.int32), live.astype(jnp.int32), parent.astype(jnp.int32))


def draw_near_index(key, part):
    return near_tables(key)[0]


def draw_near_mask(key, part):
    return near_tables(key)[1]


def draw_parent_map(key, part):
    return near_tables(key)[2]


def draw_diag_block(key, part):
    key_raw, key_diag = jax.random.split(jax.random.fold_in(key, 11), 2)
    raw = jax.random.normal(key_raw, (CLUSTERS, LEAF, LEAF), jnp.float32) / jnp.sqrt(jnp.float32(LEAF))
    symmetric = 0.5 * (raw + jnp.swapaxes(raw, 1, 2))
    diagonal = jax.random.uniform(key_diag, (CLUSTERS, LEAF), jnp.float32, 2.0, 4.0)
    matrix = symmetric + diagonal[:, :, None] * jnp.eye(LEAF, dtype=jnp.float32)[None, :, :]
    return matrix


def draw_bases(key, part):
    key_raw, key_diag = jax.random.split(jax.random.fold_in(key, 23), 2)
    noise = 0.35 * jax.random.normal(key_raw, (CLUSTERS, LEAF, LEAF), jnp.float32)
    diagonal = jax.random.uniform(key_diag, (CLUSTERS, LEAF), jnp.float32, 1.0, 2.0)
    return noise / jnp.sqrt(jnp.float32(LEAF)) + diagonal[:, :, None] * jnp.eye(LEAF, dtype=jnp.float32)[None, :, :]


def steps_of(own_key, extent, shards, smallest, top_value):
    def one(dim, blocks):
        draws = jax.random.uniform(jax.random.fold_in(jax.random.fold_in(own_key, 6), dim), (blocks,), jnp.float32, smallest / len(shards), top_value / len(shards))
        return jnp.repeat(jnp.exp(draws), extent[dim] // blocks).reshape((-1,) + (1,) * (len(extent) - dim - 1))

    level = one(*shards[0])
    for cut in shards[1:]:
        level = level * one(*cut)
    return level


def gaussian(rng, shape, width, limit, cuts=(), kind=jnp.bfloat16):
    factor_of = steps_of(rng, shape, cuts, -0.22, 0.18) if cuts else 1.0
    values = jax.random.normal(rng, shape, jnp.float32) * width * factor_of
    return jnp.minimum(jnp.maximum(values, -limit), limit).astype(kind)


def setup_inputs(seed: int = 0) -> dict:
    splits = jax.random.split(jax.random.key(seed), 7)
    near_blocks = gaussian(splits[0], (CLUSTERS, NEAR, LEAF, LEAF), LEAF ** -0.5, 0.25, ((0, 16), (1, 2)), jnp.float32)
    diag_block = draw_diag_block(jax.random.fold_in(splits[6], 71), 0)
    bases = draw_bases(jax.random.fold_in(splits[6], 71), 0)
    near_index = draw_near_index(jax.random.fold_in(splits[6], 71), 0)
    near_mask = draw_near_mask(jax.random.fold_in(splits[6], 71), 0)
    parent_map = draw_parent_map(jax.random.fold_in(splits[6], 71), 0)
    return dict(near_blocks=near_blocks, diag_block=diag_block, bases=bases, near_index=near_index, near_mask=near_mask, parent_map=parent_map)


def solve_lower(factor):
    size = factor.shape[0]
    return lax.linalg.triangular_solve(factor, jnp.eye(size, dtype=factor.dtype), left_side=True, lower=True)

def reference(near_blocks, diag_block, bases, near_index, near_mask, parent_map):
    highest = lax.Precision.HIGHEST
    count = parent_map.shape[0]
    cluster_ids = jnp.arange(count, dtype=jnp.int32)
    same = (parent_map[:, None] == parent_map[None, :]) & (cluster_ids[:, None] != cluster_ids[None, :])
    sibling = jnp.sum(jnp.where(same, cluster_ids[None, :], 0), axis=1).astype(jnp.int32)
    skeleton = bases[:, :, RED:]

    def one_cluster(inputs):
        blocks, diagonal, basis, listed, live, partner, own = inputs
        reduced = jnp.dot(basis.T, jnp.dot(diagonal, basis, precision=highest), precision=highest)
        factor = jnp.linalg.cholesky(reduced[:RED, :RED])
        inverse = solve_lower(factor)
        couple = jnp.dot(inverse, reduced[:RED, RED:], precision=highest)
        schur = reduced[RED:, RED:] - jnp.dot(couple.T, couple, precision=highest)
        partners = skeleton[listed]
        middle = jnp.einsum('kab,kbr->kar', blocks, partners, precision=highest)
        coupled = jnp.einsum('ba,kbr->kar', basis, middle, precision=highest)
        solved = jnp.einsum('xy,kyr->kxr', inverse, coupled[:, :RED], precision=highest)
        weights = live.astype(jnp.float32)
        coupling = (coupled[:, RED:] - jnp.einsum('xs,kxr->ksr', couple, solved, precision=highest)) * weights[:, None, None]
        matches = weights * (listed == partner).astype(jnp.float32)
        side = jnp.einsum('k,kab->ab', matches, coupling, precision=highest)
        first = (own < partner).astype(jnp.float32)
        merged = jnp.concatenate([first * schur + (1.0 - first) * side, (1.0 - first) * schur + first * side], axis=1)
        return (coupling, merged, factor)
    coupling, parent_rows, redundant_factor = lax.map(one_cluster, (near_blocks, diag_block, bases, near_index, near_mask, sibling, cluster_ids))
    return (coupling, parent_rows, redundant_factor)
```

```python
import functools

import jax
import jax.numpy as jnp
from jax import lax
from jax.experimental import pallas as pl
from jax.experimental.pallas import tpu as pltpu
from jax.sharding import PartitionSpec as P

RANK = 256


def solve_lower(factor):
    size = factor.shape[0]
    return lax.linalg.triangular_solve(
        factor, jnp.eye(size, dtype=factor.dtype), left_side=True, lower=True
    )


def pick_rows(listed, carry, piece):
    count = piece.shape[0]
    select = (listed[:, None] == jnp.arange(count, dtype=jnp.int32)[None, :]).astype(jnp.float32)
    flat = piece.reshape(count, -1)
    return jnp.dot(select, flat, precision=lax.Precision.HIGHEST).reshape(carry.shape)


def shards(near_blocks, diag_block, bases, near_index, near_mask, parent_map):
    highest = lax.Precision.HIGHEST
    columns = lax.axis_size("col")
    column = lax.axis_index("col")
    own_index = lax.axis_index("clu")
    row_count = bases.shape[1]
    leaf_size = bases.shape[2]
    redundant = leaf_size - RANK
    per_device = near_blocks.shape[1]
    slot_total = near_index.shape[1]
    listed = lax.dynamic_slice_in_dim(near_index, own_index, 1, 0)[0]
    full_diag, full_basis = (
        lax.all_gather(diag_block, "col", axis=1, tiled=True),
        lax.all_gather(bases, "col", axis=1, tiled=True),
    )
    basis = full_basis[0]
    reduced = jnp.dot(basis.T, jnp.dot(full_diag[0], basis, precision=highest), precision=highest)
    factor = jnp.linalg.cholesky(reduced[:redundant, :redundant])
    inverse = solve_lower(factor)
    couple = jnp.dot(inverse, reduced[:redundant, redundant:], precision=highest)
    schur = reduced[redundant:, redundant:] - jnp.dot(couple.T, couple, precision=highest)
    skeleton_rows = bases[:, :, redundant:]
    empty = jnp.zeros((slot_total, row_count, RANK), jnp.float32)
    picked = pick_rows(listed, empty, lax.all_gather(skeleton_rows, "clu", axis=0, tiled=True))
    grouped = picked.reshape(columns, per_device, row_count, RANK)
    routed = lax.all_to_all(grouped, "col", split_axis=0, concat_axis=2, tiled=True)
    partners = routed[0]
    middle = jnp.einsum("kab,kbr->kar", near_blocks[0], partners, precision=highest)
    coupled = jnp.einsum("ba,kbr->kar", basis, middle, precision=highest)
    solved = jnp.einsum("xy,kyr->kxr", inverse, coupled[:, :redundant], precision=highest)
    local_list = lax.dynamic_slice_in_dim(listed, column * per_device, per_device, 0)
    local_live = lax.dynamic_slice_in_dim(near_mask[0], column * per_device, per_device, 0).astype(
        jnp.float32
    )
    coupling = (
        coupled[:, redundant:] - jnp.einsum("xs,kxr->ksr", couple, solved, precision=highest)
    ) * local_live[:, None, None]
    cluster_ids = jnp.arange(parent_map.shape[0], dtype=jnp.int32)
    own_parent = lax.dynamic_slice_in_dim(parent_map, own_index, 1, 0)[0]
    same = (parent_map == own_parent) & (cluster_ids != own_index)
    sibling = jnp.sum(jnp.where(same, cluster_ids, 0))
    matches = local_live * (local_list == sibling).astype(jnp.float32)
    side = jnp.einsum("k,kab->ab", matches, coupling, precision=highest)
    first = (own_index < sibling).astype(jnp.float32)
    side_wide = jnp.concatenate([(1.0 - first) * side, first * side], axis=1)
    summed = lax.psum_scatter(side_wide, "col", scatter_dimension=0, tiled=True)
    merged_count = summed.shape[0]
    schur_rows = lax.dynamic_slice_in_dim(schur, column * merged_count, merged_count, 0)
    parent_rows = summed + jnp.concatenate([first * schur_rows, (1.0 - first) * schur_rows], axis=1)
    factor_count = redundant // columns
    factor_rows = lax.dynamic_slice_in_dim(factor, column * factor_count, factor_count, 0)
    return (coupling[None], parent_rows[None], factor_rows[None])


ORDERS = (("z", "x", "y", "core"), ("z", "y", "x", "core"))
DIMS = ("z", "y", "core", "x")
HIGHEST = lax.Precision.HIGHEST
BLOCK = 64


def dot(a, b, contract=((1,), (0,))):
    return lax.dot_general(
        a, b, (contract, ((), ())), precision=HIGHEST, preferred_element_type=jnp.float32
    )


def halves(x):
    high = x.astype(jnp.bfloat16)
    return high, (x - high.astype(jnp.float32)).astype(jnp.bfloat16)


def dot_split(a, b):
    one = functools.partial(jnp.dot, preferred_element_type=jnp.float32)
    return one(a[0], b[0]) + (one(a[0], b[1]) + one(a[1], b[0]))


def fused(
    clusters,
    near_ref, diag_ref, bases_ref, index_ref, mask_ref, parent_ref,
    coupling_ref, rows_ref, factor_ref,
    every, near, peer_diag, peer_red, basis, system, small, t_high, t_low, wide, lower, schur,
    w_scr, side_out, side_in,
    send_sem, recv_sem, near_sem, pair_send, pair_recv,
):
    sizes = {"z": clusters // 4, "y": 2, "core": 2, "x": 2}
    clu, col = lax.axis_index("clu"), lax.axis_index("col")
    here = {"z": clu // 4, "y": lax.rem(clu // 2, 2), "core": lax.rem(clu, 2), "x": col}
    rows = bases_ref.shape[1]
    leaf = bases_ref.shape[2]
    red = leaf - RANK
    slots = near_ref.shape[1]
    parts = ((0, rows * 3 // 4), (rows * 3 // 4, rows - rows * 3 // 4))

    def place(coords):
        return ((coords["z"] * 2 + coords["y"]) * 2 + coords["core"], coords["x"])

    def moved(rel, sign):
        return place({
            d: here[d] if rel[i] == 0 else lax.rem(here[d] + (rel[i] * sign) % sizes[d], sizes[d])
            for i, d in enumerate(DIMS)
        })

    def number(rel):
        total = 0
        for d, r in zip(DIMS, rel):
            total = total * sizes[d] + r
        return total

    zero = (0, 0, 0, 0)

    def transfer(part, source, rel):
        step = tuple(b - a for a, b in zip(source, rel))
        origin = moved(source, -1)
        start, count = parts[part]
        piece = every.at[origin[0], pl.ds(pl.multiple_of(origin[1] * rows + start, 8), count)]
        return pltpu.make_async_remote_copy(
            src_ref=piece, dst_ref=piece,
            send_sem=send_sem.at[part, number(rel)], recv_sem=recv_sem.at[part, number(rel)],
            device_id=moved(step, 1), device_id_type=pl.DeviceIdType.MESH,
        )

    def arrival(part, rel):
        origin = moved(rel, -1)
        start, count = parts[part]
        piece = every.at[origin[0], pl.ds(pl.multiple_of(origin[1] * rows + start, 8), count)]
        step = tuple((1 if d == "x" else 0) for d in DIMS)
        return pltpu.make_async_remote_copy(
            src_ref=piece, dst_ref=piece,
            send_sem=send_sem.at[part, number(rel)], recv_sem=recv_sem.at[part, number(rel)],
            device_id=moved(step, 1), device_id_type=pl.DeviceIdType.MESH,
        )

    sent = []

    def children(part, rel):
        order = ORDERS[part]
        last = max([order.index(d) for d, r in zip(DIMS, rel) if r], default=-1)
        out = []
        for d in order[last + 1:]:
            for k in range(1, sizes[d]):
                out.append((d, tuple(k if e == d else r for e, r in zip(DIMS, rel))))
        return out

    def forward(part, rel, only=None):
        for d, child in children(part, rel):
            if only is None or d in only:
                copy = transfer(part, rel, child)
                copy.start()
                sent.append(copy)

    def pump(items):
        for part, rel in items:
            arrival(part, rel).wait_recv()
            forward(part, rel)

    unit = lambda d, k: tuple(k if e == d else 0 for e in DIMS)
    peers = [unit(d, k) for d in DIMS for k in range(1, sizes[d])]

    for k in range(slots):
        pltpu.make_async_copy(near_ref.at[0, k], near.at[k], near_sem.at[k]).start()

    barrier = pltpu.get_barrier_semaphore()
    for rel in peers:
        pl.semaphore_signal(barrier, inc=1, device_id=moved(rel, 1), device_id_type=pl.DeviceIdType.MESH)
    every[clu, pl.ds(pl.multiple_of(col * rows, 8), rows), :] = bases_ref[0, :, red:]
    pl.semaphore_wait(barrier, len(peers))

    across = moved(unit("x", 1), 1)

    def pair(i, src, dst):
        return pltpu.make_async_remote_copy(
            src_ref=src, dst_ref=dst, send_sem=pair_send.at[i], recv_sem=pair_recv.at[i],
            device_id=across, device_id_type=pl.DeviceIdType.MESH,
        )

    red_copy = pair(0, bases_ref.at[0, :, pl.ds(0, red)], peer_red)
    diag_copy = pair(
        1, diag_ref.at[0, :, pl.ds(pl.multiple_of(col * rows, 128), rows)], peer_diag
    )
    red_copy.start()
    diag_copy.start()
    for part in range(2):
        forward(part, zero, ("x",))
    for part in range(2):
        forward(part, zero, ("z", "y", "core"))

    plain = [
        (part, rel)
        for rel in [
            (z, y, 0, x) for z in range(sizes["z"]) for y in range(2) for x in range(2)
        ]
        for part in range(2)
        if any(rel)
    ]
    level = lambda item: sum(1 for r in item[1] if r)
    ones = sorted([i for i in plain if level(i) == 1], key=lambda i: (-i[1][3], i[1][1]))
    twos = [i for i in plain if level(i) == 2]
    threes = [i for i in plain if level(i) == 3]

    red_copy.wait_recv()
    diag_copy.wait_recv()
    pump(ones)
    basis[:rows] = bases_ref[0]
    basis[rows:, :red] = peer_red[...]
    basis[rows:, red:] = every[clu, pl.ds(pl.multiple_of((1 - col) * rows, 8), rows), :]
    own = diag_ref[0, :, pl.ds(pl.multiple_of(col * rows, 128), rows)]
    off = diag_ref[0, :, pl.ds(pl.multiple_of((1 - col) * rows, 128), rows)]
    wide[:rows] = dot(own, basis[:rows]) + dot(off, basis[rows:])
    wide[rows:] = dot(off.T, basis[:rows]) + dot(peer_diag[...], basis[rows:])
    system[:, : red + RANK] = dot(basis[:, :red], wide[...], ((0,), (0,)))
    schur[...] = dot(basis[:, red:], wide[:, red:], ((0,), (0,)))
    row_id = lax.broadcasted_iota(jnp.int32, (red, red), 0)
    col_id = lax.broadcasted_iota(jnp.int32, (red, red), 1)
    system[:, red + RANK:] = (row_id == col_id).astype(jnp.float32)

    steps = red // BLOCK
    share = -(-len(twos) // steps)
    sub = lax.broadcasted_iota(jnp.int32, (BLOCK, 2 * BLOCK), 0)
    lane = lax.broadcasted_iota(jnp.int32, (BLOCK, 2 * BLOCK), 1)
    unit_right = (sub + BLOCK == lane).astype(jnp.float32)
    for b in range(steps):
        low, high = b * BLOCK, (b + 1) * BLOCK
        small[...] = jnp.concatenate(
            [system[low:high, low:high], unit_right[:, BLOCK:]], axis=1
        )

        def eliminate(j, _):
            block = small[...]
            row = small[pl.ds(j, 1), :]
            column = jnp.sum(jnp.where(lane == j, block, 0.0), axis=1, keepdims=True)
            pivot = jnp.sum(jnp.where(lane[:1] == j, row, 0.0), axis=1, keepdims=True)
            scaled = row / pivot
            small[...] = block - jnp.where(sub > j, column, 0.0) * scaled
            return 0

        lax.fori_loop(0, BLOCK, eliminate, 0)
        done = small[...]
        pivots = jnp.sum(jnp.where(sub == lane, done, 0.0), axis=1, keepdims=True)
        inverse = done[:, BLOCK:] / jnp.sqrt(pivots)
        solved = dot(inverse, system[low:high, :])
        upper = jnp.where(
            col_id[low:high] >= row_id[low:high], solved[:, :red], 0.0
        )
        system[low:high, :red] = upper
        system[low:high, red:] = solved[:, red:]
        if high < red:
            system[high:, :] -= dot(
                upper[:, high:], jnp.concatenate([upper, solved[:, red:]], axis=1), ((0,), (0,))
            )
        pump(twos[b * share:(b + 1) * share])
    pump(threes)

    lower[...] = system[:, :red].T
    half = red // 2
    factor_ref[0] = lower[pl.ds(pl.multiple_of(col * half, 8), half), :]
    couple = system[:, red:red + RANK]
    schur[...] -= dot(couple, couple, ((0,), (0,)))
    middle = dot(system[:, red + RANK:], couple, ((0,), (0,)))
    w_scr[pl.ds(pl.multiple_of(col * rows, 8), rows), :] = (
        basis[:rows, red:] - dot(basis[:rows, :red], middle)
    )
    w_scr[pl.ds(pl.multiple_of((1 - col) * rows, 8), rows), :] = (
        basis[rows:, red:] - dot(basis[rows:, :red], middle)
    )
    turned = halves(w_scr[...].T)

    parent = parent_ref[clu]
    sibling = jnp.int32(0)
    for c in range(clusters):
        sibling = jnp.where((parent_ref[c] == parent) & (c != clu), jnp.int32(c), sibling)

    wide[:RANK] = jnp.zeros((RANK, leaf), jnp.float32)
    for k in range(slots):
        pltpu.make_async_copy(near_ref.at[0, k], near.at[k], near_sem.at[k]).wait()

    def project(k, _):
        value = dot_split(turned, halves(near[k]))
        t_high[k], t_low[k] = halves(value)
        slot = col * slots + k
        match = jnp.where(index_ref[clu, slot] == sibling, mask_ref[0, slot], 0)
        wide[:RANK] += value * match.astype(jnp.float32)
        return 0

    lax.fori_loop(0, slots, project, 0)

    for part in range(2):
        for rel in [(z, y, 1, x) for z in range(sizes["z"]) for y in range(2) for x in range(2)]:
            arrival(part, rel).wait_recv()
    side = dot_split(halves(wide[:RANK]), halves(every[sibling]))
    quarter = RANK // 2
    side_out[...] = side
    side_copy = pair(
        2, side_out.at[pl.ds(pl.multiple_of((1 - col) * quarter, 8), quarter)], side_in
    )
    side_copy.start()

    def finish(k, _):
        slot = col * slots + k
        live = mask_ref[0, slot].astype(jnp.float32)
        coupling_ref[0, k] = live * dot_split(
            (t_high[k], t_low[k]), halves(every[index_ref[clu, slot]])
        )
        return 0

    lax.fori_loop(0, slots, finish, 0)
    side_copy.wait_recv()
    mine = pl.ds(pl.multiple_of(col * quarter, 8), quarter)
    side_rows = side_out[mine, :] + side_in[...]
    schur_rows = schur[mine, :]
    first = (clu < sibling).astype(jnp.float32)
    rows_ref[0, :, :RANK] = first * schur_rows + (1.0 - first) * side_rows
    rows_ref[0, :, RANK:] = (1.0 - first) * schur_rows + first * side_rows
    for copy in sent + [red_copy, diag_copy, side_copy]:
        copy.wait_send()


def fused_shards(near_blocks, diag_block, bases, near_index, near_mask, parent_map):
    clusters = parent_map.shape[0]
    rows, leaf = bases.shape[1:]
    red = leaf - RANK
    slots = near_blocks.shape[1]
    f32, b16 = jnp.float32, jnp.bfloat16
    vmem = pl.BlockSpec(memory_space=pltpu.VMEM)
    smem = pl.BlockSpec(memory_space=pltpu.SMEM)
    dma = pltpu.SemaphoreType.DMA
    devices = clusters * 2
    return pl.pallas_call(
        functools.partial(fused, clusters),
        out_shape=(
            jax.ShapeDtypeStruct((1, slots, RANK, RANK), f32),
            jax.ShapeDtypeStruct((1, RANK // 2, 2 * RANK), f32),
            jax.ShapeDtypeStruct((1, red // 2, red), f32),
        ),
        in_specs=[pl.BlockSpec(memory_space=pl.ANY), vmem, vmem, smem, smem, smem],
        out_specs=(vmem, vmem, vmem),
        scratch_shapes=[
            pltpu.VMEM((clusters, leaf, RANK), f32),
            pltpu.VMEM((slots, leaf, leaf), f32),
            pltpu.VMEM((rows, rows), f32),
            pltpu.VMEM((rows, red), f32),
            pltpu.VMEM((leaf, leaf), f32),
            pltpu.VMEM((red, 2 * red + RANK), f32),
            pltpu.VMEM((BLOCK, 2 * BLOCK), f32),
            pltpu.VMEM((slots, RANK, leaf), b16),
            pltpu.VMEM((slots, RANK, leaf), b16),
            pltpu.VMEM((leaf, leaf), f32),
            pltpu.VMEM((red, red), f32),
            pltpu.VMEM((RANK, RANK), f32),
            pltpu.VMEM((leaf, RANK), f32),
            pltpu.VMEM((RANK, RANK), f32),
            pltpu.VMEM((RANK // 2, RANK), f32),
            dma((2, devices)),
            dma((2, devices)),
            dma((slots,)),
            dma((3,)),
            dma((3,)),
        ],
        compiler_params=pltpu.CompilerParams(
            collective_id=0, has_side_effects=True, vmem_limit_bytes=48 * 1024 * 1024
        ),
    )(near_blocks, diag_block, bases, near_index, near_mask, parent_map)


def solution(mesh):
    in_specs = (
        P("clu", "col", None, None),
        P("clu", "col", None),
        P("clu", "col", None),
        P(),
        P("clu", None),
        P(),
    )
    out_specs = (P("clu", "col", None, None), P("clu", "col", None), P("clu", "col", None))
    pairs = mesh.shape["col"] == 2 and mesh.shape["clu"] % 4 == 0
    body = fused_shards if pairs else shards
    return jax.shard_map(body, mesh=mesh, in_specs=in_specs, out_specs=out_specs, check_vma=False)
```

```python
import functools

import jax
import jax.numpy as jnp
from jax import lax
from jax.experimental import pallas as pl
from jax.experimental.pallas import tpu as pltpu
from jax.sharding import PartitionSpec as P

RANK = 256


def solve_lower(factor):
    size = factor.shape[0]
    return lax.linalg.triangular_solve(
        factor, jnp.eye(size, dtype=factor.dtype), left_side=True, lower=True
    )


def pick_rows(listed, carry, piece):
    count = piece.shape[0]
    select = (listed[:, None] == jnp.arange(count, dtype=jnp.int32)[None, :]).astype(jnp.float32)
    flat = piece.reshape(count, -1)
    return jnp.dot(select, flat, precision=lax.Precision.HIGHEST).reshape(carry.shape)


def shards(near_blocks, diag_block, bases, near_index, near_mask, parent_map):
    highest = lax.Precision.HIGHEST
    columns = lax.axis_size("col")
    column = lax.axis_index("col")
    own_index = lax.axis_index("clu")
    row_count = bases.shape[1]
    leaf_size = bases.shape[2]
    redundant = leaf_size - RANK
    per_device = near_blocks.shape[1]
    slot_total = near_index.shape[1]
    listed = lax.dynamic_slice_in_dim(near_index, own_index, 1, 0)[0]
    full_diag, full_basis = (
        lax.all_gather(diag_block, "col", axis=1, tiled=True),
        lax.all_gather(bases, "col", axis=1, tiled=True),
    )
    basis = full_basis[0]
    reduced = jnp.dot(basis.T, jnp.dot(full_diag[0], basis, precision=highest), precision=highest)
    factor = jnp.linalg.cholesky(reduced[:redundant, :redundant])
    inverse = solve_lower(factor)
    couple = jnp.dot(inverse, reduced[:redundant, redundant:], precision=highest)
    schur = reduced[redundant:, redundant:] - jnp.dot(couple.T, couple, precision=highest)
    skeleton_rows = bases[:, :, redundant:]
    empty = jnp.zeros((slot_total, row_count, RANK), jnp.float32)
    picked = pick_rows(listed, empty, lax.all_gather(skeleton_rows, "clu", axis=0, tiled=True))
    grouped = picked.reshape(columns, per_device, row_count, RANK)
    routed = lax.all_to_all(grouped, "col", split_axis=0, concat_axis=2, tiled=True)
    partners = routed[0]
    middle = jnp.einsum("kab,kbr->kar", near_blocks[0], partners, precision=highest)
    coupled = jnp.einsum("ba,kbr->kar", basis, middle, precision=highest)
    solved = jnp.einsum("xy,kyr->kxr", inverse, coupled[:, :redundant], precision=highest)
    local_list = lax.dynamic_slice_in_dim(listed, column * per_device, per_device, 0)
    local_live = lax.dynamic_slice_in_dim(near_mask[0], column * per_device, per_device, 0).astype(
        jnp.float32
    )
    coupling = (
        coupled[:, redundant:] - jnp.einsum("xs,kxr->ksr", couple, solved, precision=highest)
    ) * local_live[:, None, None]
    cluster_ids = jnp.arange(parent_map.shape[0], dtype=jnp.int32)
    own_parent = lax.dynamic_slice_in_dim(parent_map, own_index, 1, 0)[0]
    same = (parent_map == own_parent) & (cluster_ids != own_index)
    sibling = jnp.sum(jnp.where(same, cluster_ids, 0))
    matches = local_live * (local_list == sibling).astype(jnp.float32)
    side = jnp.einsum("k,kab->ab", matches, coupling, precision=highest)
    first = (own_index < sibling).astype(jnp.float32)
    side_wide = jnp.concatenate([(1.0 - first) * side, first * side], axis=1)
    summed = lax.psum_scatter(side_wide, "col", scatter_dimension=0, tiled=True)
    merged_count = summed.shape[0]
    schur_rows = lax.dynamic_slice_in_dim(schur, column * merged_count, merged_count, 0)
    parent_rows = summed + jnp.concatenate([first * schur_rows, (1.0 - first) * schur_rows], axis=1)
    factor_count = redundant // columns
    factor_rows = lax.dynamic_slice_in_dim(factor, column * factor_count, factor_count, 0)
    return (coupling[None], parent_rows[None], factor_rows[None])


ORDERS = (("z", "x", "y", "core"), ("z", "y", "x", "core"))
DIMS = ("z", "y", "core", "x")
HIGHEST = lax.Precision.HIGHEST
BLOCK = 64


def dot(a, b, contract=((1,), (0,))):
    return lax.dot_general(
        a, b, (contract, ((), ())), precision=HIGHEST, preferred_element_type=jnp.float32
    )


def halves(x):
    high = x.astype(jnp.bfloat16)
    return high, (x - high.astype(jnp.float32)).astype(jnp.bfloat16)


def dot_split(a, b):
    one = functools.partial(jnp.dot, preferred_element_type=jnp.float32)
    return one(a[0], b[0]) + (one(a[0], b[1]) + one(a[1], b[0]))


def fused(
    clusters,
    near_ref, diag_ref, bases_ref, index_ref, mask_ref, parent_ref,
    coupling_ref, rows_ref, factor_ref,
    every, near, peer_diag, peer_red, basis, system, t_high, t_low, wide, lower, schur,
    w_scr, side_out, side_in,
    send_sem, recv_sem, near_sem, pair_send, pair_recv,
):
    sizes = {"z": clusters // 4, "y": 2, "core": 2, "x": 2}
    clu, col = lax.axis_index("clu"), lax.axis_index("col")
    here = {"z": clu // 4, "y": lax.rem(clu // 2, 2), "core": lax.rem(clu, 2), "x": col}
    rows = bases_ref.shape[1]
    leaf = bases_ref.shape[2]
    red = leaf - RANK
    slots = near_ref.shape[1]
    parts = ((0, rows * 3 // 4), (rows * 3 // 4, rows - rows * 3 // 4))

    def place(coords):
        return ((coords["z"] * 2 + coords["y"]) * 2 + coords["core"], coords["x"])

    def moved(rel, sign):
        return place({
            d: here[d] if rel[i] == 0 else lax.rem(here[d] + (rel[i] * sign) % sizes[d], sizes[d])
            for i, d in enumerate(DIMS)
        })

    def number(rel):
        total = 0
        for d, r in zip(DIMS, rel):
            total = total * sizes[d] + r
        return total

    zero = (0, 0, 0, 0)

    def transfer(part, source, rel):
        step = tuple(b - a for a, b in zip(source, rel))
        origin = moved(source, -1)
        start, count = parts[part]
        piece = every.at[origin[0], pl.ds(pl.multiple_of(origin[1] * rows + start, 8), count)]
        return pltpu.make_async_remote_copy(
            src_ref=piece, dst_ref=piece,
            send_sem=send_sem.at[part, number(rel)], recv_sem=recv_sem.at[part, number(rel)],
            device_id=moved(step, 1), device_id_type=pl.DeviceIdType.MESH,
        )

    def arrival(part, rel):
        origin = moved(rel, -1)
        start, count = parts[part]
        piece = every.at[origin[0], pl.ds(pl.multiple_of(origin[1] * rows + start, 8), count)]
        step = tuple((1 if d == "x" else 0) for d in DIMS)
        return pltpu.make_async_remote_copy(
            src_ref=piece, dst_ref=piece,
            send_sem=send_sem.at[part, number(rel)], recv_sem=recv_sem.at[part, number(rel)],
            device_id=moved(step, 1), device_id_type=pl.DeviceIdType.MESH,
        )

    sent = []

    def children(part, rel):
        order = ORDERS[part]
        last = max([order.index(d) for d, r in zip(DIMS, rel) if r], default=-1)
        out = []
        for d in order[last + 1:]:
            for k in range(1, sizes[d]):
                out.append((d, tuple(k if e == d else r for e, r in zip(DIMS, rel))))
        return out

    def forward(part, rel, only=None):
        for d, child in children(part, rel):
            if only is None or d in only:
                copy = transfer(part, rel, child)
                copy.start()
                sent.append(copy)

    def pump(items):
        for part, rel in items:
            arrival(part, rel).wait_recv()
            forward(part, rel)

    unit = lambda d, k: tuple(k if e == d else 0 for e in DIMS)
    peers = [unit(d, k) for d in DIMS for k in range(1, sizes[d])]

    for k in range(slots):
        pltpu.make_async_copy(near_ref.at[0, k], near.at[k], near_sem.at[k]).start()

    barrier = pltpu.get_barrier_semaphore()
    for rel in peers:
        pl.semaphore_signal(barrier, inc=1, device_id=moved(rel, 1), device_id_type=pl.DeviceIdType.MESH)
    every[clu, pl.ds(pl.multiple_of(col * rows, 8), rows), :] = bases_ref[0, :, red:]
    pl.semaphore_wait(barrier, len(peers))

    across = moved(unit("x", 1), 1)

    def pair(i, src, dst):
        return pltpu.make_async_remote_copy(
            src_ref=src, dst_ref=dst, send_sem=pair_send.at[i], recv_sem=pair_recv.at[i],
            device_id=across, device_id_type=pl.DeviceIdType.MESH,
        )

    red_copy = pair(0, bases_ref.at[0, :, pl.ds(0, red)], peer_red)
    diag_copy = pair(
        1, diag_ref.at[0, :, pl.ds(pl.multiple_of(col * rows, 128), rows)], peer_diag
    )
    red_copy.start()
    diag_copy.start()
    for part in range(2):
        forward(part, zero, ("x",))
    for part in range(2):
        forward(part, zero, ("z", "y", "core"))

    plain = [
        (part, rel)
        for rel in [
            (z, y, 0, x) for z in range(sizes["z"]) for y in range(2) for x in range(2)
        ]
        for part in range(2)
        if any(rel)
    ]
    level = lambda item: sum(1 for r in item[1] if r)
    ones = sorted([i for i in plain if level(i) == 1], key=lambda i: (-i[1][3], i[1][1]))
    twos = [i for i in plain if level(i) == 2]
    threes = [i for i in plain if level(i) == 3]

    red_copy.wait_recv()
    diag_copy.wait_recv()
    pump(ones)
    basis[:rows] = bases_ref[0]
    basis[rows:, :red] = peer_red[...]
    basis[rows:, red:] = every[clu, pl.ds(pl.multiple_of((1 - col) * rows, 8), rows), :]
    own = diag_ref[0, :, pl.ds(pl.multiple_of(col * rows, 128), rows)]
    off = diag_ref[0, :, pl.ds(pl.multiple_of((1 - col) * rows, 128), rows)]
    wide[:rows] = dot(own, basis[:rows]) + dot(off, basis[rows:])
    wide[rows:] = dot(off.T, basis[:rows]) + dot(peer_diag[...], basis[rows:])
    system[:, : red + RANK] = dot(basis[:, :red], wide[...], ((0,), (0,)))
    schur[...] = dot(basis[:, red:], wide[:, red:], ((0,), (0,)))
    row_id = lax.broadcasted_iota(jnp.int32, (red, red), 0)
    col_id = lax.broadcasted_iota(jnp.int32, (red, red), 1)
    system[:, red + RANK:] = (row_id == col_id).astype(jnp.float32)

    steps = red // BLOCK
    share = -(-len(twos) // steps)
    sub = lax.broadcasted_iota(jnp.int32, (BLOCK, 2 * BLOCK), 0)
    lane = lax.broadcasted_iota(jnp.int32, (BLOCK, 2 * BLOCK), 1)
    unit_right = (sub + BLOCK == lane).astype(jnp.float32)
    for b in range(steps):
        low, high = b * BLOCK, (b + 1) * BLOCK
        done = jnp.concatenate([system[low:high, low:high], unit_right[:, BLOCK:]], axis=1)
        for j in range(BLOCK - 1):
            column = done[:, j:j + 1]
            scaled = done[j:j + 1, :] / done[j:j + 1, j:j + 1]
            done = done - jnp.where(sub > j, column, 0.0) * scaled
        pivots = jnp.sum(jnp.where(sub == lane, done, 0.0), axis=1, keepdims=True)
        inverse = done[:, BLOCK:] / jnp.sqrt(pivots)
        solved = dot(inverse, system[low:high, :])
        upper = jnp.where(
            col_id[low:high] >= row_id[low:high], solved[:, :red], 0.0
        )
        system[low:high, :red] = upper
        system[low:high, red:] = solved[:, red:]
        if high < red:
            system[high:, :] -= dot(
                upper[:, high:], jnp.concatenate([upper, solved[:, red:]], axis=1), ((0,), (0,))
            )
        pump(twos[b * share:(b + 1) * share])
    pump(threes)

    lower[...] = system[:, :red].T
    half = red // 2
    factor_ref[0] = lower[pl.ds(pl.multiple_of(col * half, 8), half), :]
    couple = system[:, red:red + RANK]
    schur[...] -= dot(couple, couple, ((0,), (0,)))
    middle = dot(system[:, red + RANK:], couple, ((0,), (0,)))
    w_scr[pl.ds(pl.multiple_of(col * rows, 8), rows), :] = (
        basis[:rows, red:] - dot(basis[:rows, :red], middle)
    )
    w_scr[pl.ds(pl.multiple_of((1 - col) * rows, 8), rows), :] = (
        basis[rows:, red:] - dot(basis[rows:, :red], middle)
    )
    turned = halves(w_scr[...].T)

    parent = parent_ref[clu]
    sibling = jnp.int32(0)
    for c in range(clusters):
        sibling = jnp.where((parent_ref[c] == parent) & (c != clu), jnp.int32(c), sibling)

    wide[:RANK] = jnp.zeros((RANK, leaf), jnp.float32)
    for k in range(slots):
        pltpu.make_async_copy(near_ref.at[0, k], near.at[k], near_sem.at[k]).wait()

    def project(k, _):
        value = dot_split(turned, halves(near[k]))
        t_high[k], t_low[k] = halves(value)
        slot = col * slots + k
        match = jnp.where(index_ref[clu, slot] == sibling, mask_ref[0, slot], 0)
        wide[:RANK] += value * match.astype(jnp.float32)
        return 0

    lax.fori_loop(0, slots, project, 0)

    for part in range(2):
        for rel in [(z, y, 1, x) for z in range(sizes["z"]) for y in range(2) for x in range(2)]:
            arrival(part, rel).wait_recv()
    side = dot_split(halves(wide[:RANK]), halves(every[sibling]))
    quarter = RANK // 2
    side_out[...] = side
    side_copy = pair(
        2, side_out.at[pl.ds(pl.multiple_of((1 - col) * quarter, 8), quarter)], side_in
    )
    side_copy.start()

    def finish(k, _):
        slot = col * slots + k
        live = mask_ref[0, slot].astype(jnp.float32)
        coupling_ref[0, k] = live * dot_split(
            (t_high[k], t_low[k]), halves(every[index_ref[clu, slot]])
        )
        return 0

    lax.fori_loop(0, slots, finish, 0)
    side_copy.wait_recv()
    mine = pl.ds(pl.multiple_of(col * quarter, 8), quarter)
    side_rows = side_out[mine, :] + side_in[...]
    schur_rows = schur[mine, :]
    first = (clu < sibling).astype(jnp.float32)
    rows_ref[0, :, :RANK] = first * schur_rows + (1.0 - first) * side_rows
    rows_ref[0, :, RANK:] = (1.0 - first) * schur_rows + first * side_rows
    for copy in sent + [red_copy, diag_copy, side_copy]:
        copy.wait_send()


def fused_shards(near_blocks, diag_block, bases, near_index, near_mask, parent_map):
    clusters = parent_map.shape[0]
    rows, leaf = bases.shape[1:]
    red = leaf - RANK
    slots = near_blocks.shape[1]
    f32, b16 = jnp.float32, jnp.bfloat16
    vmem = pl.BlockSpec(memory_space=pltpu.VMEM)
    smem = pl.BlockSpec(memory_space=pltpu.SMEM)
    dma = pltpu.SemaphoreType.DMA
    devices = clusters * 2
    return pl.pallas_call(
        functools.partial(fused, clusters),
        out_shape=(
            jax.ShapeDtypeStruct((1, slots, RANK, RANK), f32),
            jax.ShapeDtypeStruct((1, RANK // 2, 2 * RANK), f32),
            jax.ShapeDtypeStruct((1, red // 2, red), f32),
        ),
        in_specs=[pl.BlockSpec(memory_space=pl.ANY), vmem, vmem, smem, smem, smem],
        out_specs=(vmem, vmem, vmem),
        scratch_shapes=[
            pltpu.VMEM((clusters, leaf, RANK), f32),
            pltpu.VMEM((slots, leaf, leaf), f32),
            pltpu.VMEM((rows, rows), f32),
            pltpu.VMEM((rows, red), f32),
            pltpu.VMEM((leaf, leaf), f32),
            pltpu.VMEM((red, 2 * red + RANK), f32),
            pltpu.VMEM((slots, RANK, leaf), b16),
            pltpu.VMEM((slots, RANK, leaf), b16),
            pltpu.VMEM((leaf, leaf), f32),
            pltpu.VMEM((red, red), f32),
            pltpu.VMEM((RANK, RANK), f32),
            pltpu.VMEM((leaf, RANK), f32),
            pltpu.VMEM((RANK, RANK), f32),
            pltpu.VMEM((RANK // 2, RANK), f32),
            dma((2, devices)),
            dma((2, devices)),
            dma((slots,)),
            dma((3,)),
            dma((3,)),
        ],
        compiler_params=pltpu.CompilerParams(
            collective_id=0, has_side_effects=True, vmem_limit_bytes=48 * 1024 * 1024
        ),
    )(near_blocks, diag_block, bases, near_index, near_mask, parent_map)


def solution(mesh):
    in_specs = (
        P("clu", "col", None, None),
        P("clu", "col", None),
        P("clu", "col", None),
        P(),
        P("clu", None),
        P(),
    )
    out_specs = (P("clu", "col", None, None), P("clu", "col", None), P("clu", "col", None))
    pairs = mesh.shape["col"] == 2 and mesh.shape["clu"] % 4 == 0
    body = fused_shards if pairs else shards
    return jax.shard_map(body, mesh=mesh, in_specs=in_specs, out_specs=out_specs, check_vma=False)
```

```python
import functools

import jax
import jax.numpy as jnp
from jax import lax
from jax.experimental import pallas as pl
from jax.experimental.pallas import tpu as pltpu
from jax.sharding import PartitionSpec as P

RANK = 256


def solve_lower(factor):
    size = factor.shape[0]
    return lax.linalg.triangular_solve(
        factor, jnp.eye(size, dtype=factor.dtype), left_side=True, lower=True
    )


def pick_rows(listed, carry, piece):
    count = piece.shape[0]
    select = (listed[:, None] == jnp.arange(count, dtype=jnp.int32)[None, :]).astype(jnp.float32)
    flat = piece.reshape(count, -1)
    return jnp.dot(select, flat, precision=lax.Precision.HIGHEST).reshape(carry.shape)


def shards(near_blocks, diag_block, bases, near_index, near_mask, parent_map):
    highest = lax.Precision.HIGHEST
    columns = lax.axis_size("col")
    column = lax.axis_index("col")
    own_index = lax.axis_index("clu")
    row_count = bases.shape[1]
    leaf_size = bases.shape[2]
    redundant = leaf_size - RANK
    per_device = near_blocks.shape[1]
    slot_total = near_index.shape[1]
    listed = lax.dynamic_slice_in_dim(near_index, own_index, 1, 0)[0]
    full_diag, full_basis = (
        lax.all_gather(diag_block, "col", axis=1, tiled=True),
        lax.all_gather(bases, "col", axis=1, tiled=True),
    )
    basis = full_basis[0]
    reduced = jnp.dot(basis.T, jnp.dot(full_diag[0], basis, precision=highest), precision=highest)
    factor = jnp.linalg.cholesky(reduced[:redundant, :redundant])
    inverse = solve_lower(factor)
    couple = jnp.dot(inverse, reduced[:redundant, redundant:], precision=highest)
    schur = reduced[redundant:, redundant:] - jnp.dot(couple.T, couple, precision=highest)
    skeleton_rows = bases[:, :, redundant:]
    empty = jnp.zeros((slot_total, row_count, RANK), jnp.float32)
    picked = pick_rows(listed, empty, lax.all_gather(skeleton_rows, "clu", axis=0, tiled=True))
    grouped = picked.reshape(columns, per_device, row_count, RANK)
    routed = lax.all_to_all(grouped, "col", split_axis=0, concat_axis=2, tiled=True)
    partners = routed[0]
    middle = jnp.einsum("kab,kbr->kar", near_blocks[0], partners, precision=highest)
    coupled = jnp.einsum("ba,kbr->kar", basis, middle, precision=highest)
    solved = jnp.einsum("xy,kyr->kxr", inverse, coupled[:, :redundant], precision=highest)
    local_list = lax.dynamic_slice_in_dim(listed, column * per_device, per_device, 0)
    local_live = lax.dynamic_slice_in_dim(near_mask[0], column * per_device, per_device, 0).astype(
        jnp.float32
    )
    coupling = (
        coupled[:, redundant:] - jnp.einsum("xs,kxr->ksr", couple, solved, precision=highest)
    ) * local_live[:, None, None]
    cluster_ids = jnp.arange(parent_map.shape[0], dtype=jnp.int32)
    own_parent = lax.dynamic_slice_in_dim(parent_map, own_index, 1, 0)[0]
    same = (parent_map == own_parent) & (cluster_ids != own_index)
    sibling = jnp.sum(jnp.where(same, cluster_ids, 0))
    matches = local_live * (local_list == sibling).astype(jnp.float32)
    side = jnp.einsum("k,kab->ab", matches, coupling, precision=highest)
    first = (own_index < sibling).astype(jnp.float32)
    side_wide = jnp.concatenate([(1.0 - first) * side, first * side], axis=1)
    summed = lax.psum_scatter(side_wide, "col", scatter_dimension=0, tiled=True)
    merged_count = summed.shape[0]
    schur_rows = lax.dynamic_slice_in_dim(schur, column * merged_count, merged_count, 0)
    parent_rows = summed + jnp.concatenate([first * schur_rows, (1.0 - first) * schur_rows], axis=1)
    factor_count = redundant // columns
    factor_rows = lax.dynamic_slice_in_dim(factor, column * factor_count, factor_count, 0)
    return (coupling[None], parent_rows[None], factor_rows[None])


ORDERS = (("z", "x", "y", "core"), ("z", "y", "x", "core"))
DIMS = ("z", "y", "core", "x")
HIGHEST = lax.Precision.HIGHEST
BLOCK = 64


def dot(a, b, contract=((1,), (0,))):
    return lax.dot_general(
        a, b, (contract, ((), ())), precision=HIGHEST, preferred_element_type=jnp.float32
    )


def halves(x):
    high = x.astype(jnp.bfloat16)
    return high, (x - high.astype(jnp.float32)).astype(jnp.bfloat16)


def dot_split(a, b):
    one = functools.partial(jnp.dot, preferred_element_type=jnp.float32)
    return one(a[0], b[0]) + (one(a[0], b[1]) + one(a[1], b[0]))


def fused(
    clusters,
    near_ref, diag_ref, bases_ref, index_ref, mask_ref, parent_ref,
    coupling_ref, rows_ref, factor_ref,
    every, near, peer_diag, peer_red, basis, system, t_high, t_low, wide, lower, schur,
    w_scr, side_out, side_in,
    send_sem, recv_sem, near_sem, pair_send, pair_recv,
):
    sizes = {"z": clusters // 4, "y": 2, "core": 2, "x": 2}
    clu, col = lax.axis_index("clu"), lax.axis_index("col")
    here = {"z": clu // 4, "y": lax.rem(clu // 2, 2), "core": lax.rem(clu, 2), "x": col}
    rows = bases_ref.shape[1]
    leaf = bases_ref.shape[2]
    red = leaf - RANK
    slots = near_ref.shape[1]
    parts = ((0, rows * 3 // 4), (rows * 3 // 4, rows - rows * 3 // 4))

    def place(coords):
        return ((coords["z"] * 2 + coords["y"]) * 2 + coords["core"], coords["x"])

    def moved(rel, sign):
        return place({
            d: here[d] if rel[i] == 0 else lax.rem(here[d] + (rel[i] * sign) % sizes[d], sizes[d])
            for i, d in enumerate(DIMS)
        })

    def number(rel):
        total = 0
        for d, r in zip(DIMS, rel):
            total = total * sizes[d] + r
        return total

    zero = (0, 0, 0, 0)

    def transfer(part, source, rel):
        step = tuple(b - a for a, b in zip(source, rel))
        origin = moved(source, -1)
        start, count = parts[part]
        piece = every.at[origin[0], pl.ds(pl.multiple_of(origin[1] * rows + start, 8), count)]
        return pltpu.make_async_remote_copy(
            src_ref=piece, dst_ref=piece,
            send_sem=send_sem.at[part, number(rel)], recv_sem=recv_sem.at[part, number(rel)],
            device_id=moved(step, 1), device_id_type=pl.DeviceIdType.MESH,
        )

    def arrival(part, rel):
        origin = moved(rel, -1)
        start, count = parts[part]
        piece = every.at[origin[0], pl.ds(pl.multiple_of(origin[1] * rows + start, 8), count)]
        step = tuple((1 if d == "x" else 0) for d in DIMS)
        return pltpu.make_async_remote_copy(
            src_ref=piece, dst_ref=piece,
            send_sem=send_sem.at[part, number(rel)], recv_sem=recv_sem.at[part, number(rel)],
            device_id=moved(step, 1), device_id_type=pl.DeviceIdType.MESH,
        )

    sent = []

    def children(part, rel):
        order = ORDERS[part]
        last = max([order.index(d) for d, r in zip(DIMS, rel) if r], default=-1)
        out = []
        for d in order[last + 1:]:
            for k in range(1, sizes[d]):
                out.append((d, tuple(k if e == d else r for e, r in zip(DIMS, rel))))
        return out

    def forward(part, rel, only=None):
        for d, child in children(part, rel):
            if only is None or d in only:
                copy = transfer(part, rel, child)
                copy.start()
                sent.append(copy)

    def pump(items):
        for part, rel in items:
            arrival(part, rel).wait_recv()
            forward(part, rel)

    unit = lambda d, k: tuple(k if e == d else 0 for e in DIMS)
    peers = [unit(d, k) for d in DIMS for k in range(1, sizes[d])]

    for k in range(slots):
        pltpu.make_async_copy(near_ref.at[0, k], near.at[k], near_sem.at[k]).start()

    barrier = pltpu.get_barrier_semaphore()
    for rel in peers:
        pl.semaphore_signal(barrier, inc=1, device_id=moved(rel, 1), device_id_type=pl.DeviceIdType.MESH)
    every[clu, pl.ds(pl.multiple_of(col * rows, 8), rows), :] = bases_ref[0, :, red:]
    pl.semaphore_wait(barrier, len(peers))

    across = moved(unit("x", 1), 1)

    def pair(i, src, dst):
        return pltpu.make_async_remote_copy(
            src_ref=src, dst_ref=dst, send_sem=pair_send.at[i], recv_sem=pair_recv.at[i],
            device_id=across, device_id_type=pl.DeviceIdType.MESH,
        )

    red_copy = pair(0, bases_ref.at[0, :, pl.ds(0, red)], peer_red)
    diag_copy = pair(
        1, diag_ref.at[0, :, pl.ds(pl.multiple_of(col * rows, 128), rows)], peer_diag
    )
    red_copy.start()
    diag_copy.start()
    for part in range(2):
        forward(part, zero, ("x",))
    for part in range(2):
        forward(part, zero, ("z", "y", "core"))

    plain = [
        (part, rel)
        for rel in [
            (z, y, 0, x) for z in range(sizes["z"]) for y in range(2) for x in range(2)
        ]
        for part in range(2)
        if any(rel)
    ]
    level = lambda item: sum(1 for r in item[1] if r)
    ones = sorted([i for i in plain if level(i) == 1], key=lambda i: (-i[1][3], i[1][1]))
    twos = [i for i in plain if level(i) == 2]
    threes = [i for i in plain if level(i) == 3]

    red_copy.wait_recv()
    diag_copy.wait_recv()
    pump(ones)
    basis[:rows] = bases_ref[0]
    basis[rows:, :red] = peer_red[...]
    basis[rows:, red:] = every[clu, pl.ds(pl.multiple_of((1 - col) * rows, 8), rows), :]
    own = diag_ref[0, :, pl.ds(pl.multiple_of(col * rows, 128), rows)]
    off = diag_ref[0, :, pl.ds(pl.multiple_of((1 - col) * rows, 128), rows)]
    wide[:rows] = dot(own, basis[:rows]) + dot(off, basis[rows:])
    wide[rows:] = dot(off.T, basis[:rows]) + dot(peer_diag[...], basis[rows:])
    system[:, : red + RANK] = dot(basis[:, :red], wide[...], ((0,), (0,)))
    schur[...] = dot(basis[:, red:], wide[:, red:], ((0,), (0,)))
    row_id = lax.broadcasted_iota(jnp.int32, (red, red), 0)
    col_id = lax.broadcasted_iota(jnp.int32, (red, red), 1)
    system[:, red + RANK:] = (row_id == col_id).astype(jnp.float32)

    steps = red // BLOCK
    share = -(-len(twos) // steps)
    sub = lax.broadcasted_iota(jnp.int32, (BLOCK, 2 * BLOCK), 0)
    lane = lax.broadcasted_iota(jnp.int32, (BLOCK, 2 * BLOCK), 1)
    unit_right = (sub + BLOCK == lane).astype(jnp.float32)
    for b in range(steps):
        low, high = b * BLOCK, (b + 1) * BLOCK
        done = jnp.concatenate([system[low:high, low:high], unit_right[:, BLOCK:]], axis=1)
        for j in range(0, BLOCK, 2):
            left = jnp.broadcast_to(done[:, j:j + 1], done.shape)
            right = jnp.broadcast_to(done[:, j + 1:j + 2], done.shape)
            pivot = left[j:j + 1, :]
            scaled = done[j:j + 1, :] / pivot
            right = right - left * (right[j:j + 1, :] / pivot)
            second = done[j + 1:j + 2, :] - left[j + 1:j + 2, :] * scaled
            second = second / right[j + 1:j + 2, :]
            done = (
                done
                - jnp.where(sub > j, left, 0.0) * scaled
                - jnp.where(sub > j + 1, right, 0.0) * second
            )
        pivots = jnp.sum(jnp.where(sub == lane, done, 0.0), axis=1, keepdims=True)
        inverse = done[:, BLOCK:] / jnp.sqrt(pivots)
        solved = dot(inverse, system[low:high, :])
        upper = jnp.where(
            col_id[low:high] >= row_id[low:high], solved[:, :red], 0.0
        )
        system[low:high, :red] = upper
        system[low:high, red:] = solved[:, red:]
        if high < red:
            system[high:, :] -= dot(
                upper[:, high:], jnp.concatenate([upper, solved[:, red:]], axis=1), ((0,), (0,))
            )
        pump(twos[b * share:(b + 1) * share])
    pump(threes)

    lower[...] = system[:, :red].T
    half = red // 2
    factor_ref[0] = lower[pl.ds(pl.multiple_of(col * half, 8), half), :]
    couple = system[:, red:red + RANK]
    schur[...] -= dot(couple, couple, ((0,), (0,)))
    middle = dot(system[:, red + RANK:], couple, ((0,), (0,)))
    w_scr[pl.ds(pl.multiple_of(col * rows, 8), rows), :] = (
        basis[:rows, red:] - dot(basis[:rows, :red], middle)
    )
    w_scr[pl.ds(pl.multiple_of((1 - col) * rows, 8), rows), :] = (
        basis[rows:, red:] - dot(basis[rows:, :red], middle)
    )
    turned = halves(w_scr[...].T)

    parent = parent_ref[clu]
    sibling = jnp.int32(0)
    for c in range(clusters):
        sibling = jnp.where((parent_ref[c] == parent) & (c != clu), jnp.int32(c), sibling)

    wide[:RANK] = jnp.zeros((RANK, leaf), jnp.float32)
    for k in range(slots):
        pltpu.make_async_copy(near_ref.at[0, k], near.at[k], near_sem.at[k]).wait()

    def project(k, _):
        value = dot_split(turned, halves(near[k]))
        t_high[k], t_low[k] = halves(value)
        slot = col * slots + k
        match = jnp.where(index_ref[clu, slot] == sibling, mask_ref[0, slot], 0)
        wide[:RANK] += value * match.astype(jnp.float32)
        return 0

    lax.fori_loop(0, slots, project, 0)

    for part in range(2):
        for rel in [(z, y, 1, x) for z in range(sizes["z"]) for y in range(2) for x in range(2)]:
            arrival(part, rel).wait_recv()
    side = dot_split(halves(wide[:RANK]), halves(every[sibling]))
    quarter = RANK // 2
    side_out[...] = side
    side_copy = pair(
        2, side_out.at[pl.ds(pl.multiple_of((1 - col) * quarter, 8), quarter)], side_in
    )
    side_copy.start()

    def finish(k, _):
        slot = col * slots + k
        live = mask_ref[0, slot].astype(jnp.float32)
        coupling_ref[0, k] = live * dot_split(
            (t_high[k], t_low[k]), halves(every[index_ref[clu, slot]])
        )
        return 0

    lax.fori_loop(0, slots, finish, 0)
    side_copy.wait_recv()
    mine = pl.ds(pl.multiple_of(col * quarter, 8), quarter)
    side_rows = side_out[mine, :] + side_in[...]
    schur_rows = schur[mine, :]
    first = (clu < sibling).astype(jnp.float32)
    rows_ref[0, :, :RANK] = first * schur_rows + (1.0 - first) * side_rows
    rows_ref[0, :, RANK:] = (1.0 - first) * schur_rows + first * side_rows
    for copy in sent + [red_copy, diag_copy, side_copy]:
        copy.wait_send()


def fused_shards(near_blocks, diag_block, bases, near_index, near_mask, parent_map):
    clusters = parent_map.shape[0]
    rows, leaf = bases.shape[1:]
    red = leaf - RANK
    slots = near_blocks.shape[1]
    f32, b16 = jnp.float32, jnp.bfloat16
    vmem = pl.BlockSpec(memory_space=pltpu.VMEM)
    smem = pl.BlockSpec(memory_space=pltpu.SMEM)
    dma = pltpu.SemaphoreType.DMA
    devices = clusters * 2
    return pl.pallas_call(
        functools.partial(fused, clusters),
        out_shape=(
            jax.ShapeDtypeStruct((1, slots, RANK, RANK), f32),
            jax.ShapeDtypeStruct((1, RANK // 2, 2 * RANK), f32),
            jax.ShapeDtypeStruct((1, red // 2, red), f32),
        ),
        in_specs=[pl.BlockSpec(memory_space=pl.ANY), vmem, vmem, smem, smem, smem],
        out_specs=(vmem, vmem, vmem),
        scratch_shapes=[
            pltpu.VMEM((clusters, leaf, RANK), f32),
            pltpu.VMEM((slots, leaf, leaf), f32),
            pltpu.VMEM((rows, rows), f32),
            pltpu.VMEM((rows, red), f32),
            pltpu.VMEM((leaf, leaf), f32),
            pltpu.VMEM((red, 2 * red + RANK), f32),
            pltpu.VMEM((slots, RANK, leaf), b16),
            pltpu.VMEM((slots, RANK, leaf), b16),
            pltpu.VMEM((leaf, leaf), f32),
            pltpu.VMEM((red, red), f32),
            pltpu.VMEM((RANK, RANK), f32),
            pltpu.VMEM((leaf, RANK), f32),
            pltpu.VMEM((RANK, RANK), f32),
            pltpu.VMEM((RANK // 2, RANK), f32),
            dma((2, devices)),
            dma((2, devices)),
            dma((slots,)),
            dma((3,)),
            dma((3,)),
        ],
        compiler_params=pltpu.CompilerParams(
            collective_id=0, has_side_effects=True, vmem_limit_bytes=48 * 1024 * 1024
        ),
    )(near_blocks, diag_block, bases, near_index, near_mask, parent_map)


def solution(mesh):
    in_specs = (
        P("clu", "col", None, None),
        P("clu", "col", None),
        P("clu", "col", None),
        P(),
        P("clu", None),
        P(),
    )
    out_specs = (P("clu", "col", None, None), P("clu", "col", None), P("clu", "col", None))
    pairs = mesh.shape["col"] == 2 and mesh.shape["clu"] % 4 == 0
    body = fused_shards if pairs else shards
    return jax.shard_map(body, mesh=mesh, in_specs=in_specs, out_specs=out_specs, check_vma=False)
```
